32 devices in a mesh: freq: 8 (over z, x), blk: 4 (over y, core).
Axes of the slice: x: 2, y: 2, z: 4, core: 2. Of those that a mesh axis runs over, the one named last changes fastest.
Arguments:
- voltages: int32 [2, 512, 65536], P(None, 'blk', 'freq'), may hold values from -8 to 7
- taps: int32 [4, 1024], replicated, may hold values from -32 to 127
Outputs:
- visibilities: float32 [2, 1024, 512, 512], P(None, 'freq', 'blk')
The draws below stay inside these ranges and needn't reach their ends.
All inputs are finite; a program needn't handle non-finite values.
Results may differ from the reference program's by a relative error of at most 0.00065.
Values may be sent and summed in bfloat16 or wider, within the bound.
No kernel may reach another device: no remote copies, remote signals or barrier semaphores. Data moves between devices by JAX's collectives and lax.ppermute only.
A program may use at most 256 MiB of HBM per device.

```python
import math
import jax
import jax.numpy as jnp
from jax import lax

C = 1024
TAPS = 4
INPUTS = 512
SPECTRA = 64
SAMPLES = 65536
N_FREQ = 8


def plant(entries, key, smallest, largest):
    index_at = [jax.random.randint(jax.random.fold_in(key, axis), (), 0, length) for axis, length in enumerate(entries.shape)]
    longest = entries.shape.index(max(entries.shape))
    next_to = index_at[:longest] + [(index_at[longest] + 1) % entries.shape[longest]] + index_at[longest + 1:]
    return entries.at[tuple(index_at)].set(smallest).at[tuple(next_to)].set(largest)


def setup_inputs(seed: int = 0) -> dict:
    seeds = jax.random.split(jax.random.key(seed), 3)
    voltages = plant(jax.random.randint(seeds[0], (2, INPUTS, SAMPLES), -8, 8), jax.random.fold_in(seeds[0], 1), -8, 7).astype(jnp.int32)
    taps = plant(jax.random.randint(seeds[1], (TAPS, C), -32, 128), jax.random.fold_in(seeds[1], 1), -32, 127).astype(jnp.int32)
    return {"voltages": voltages, "taps": taps}


def dft_table(channels):
    row_index = lax.broadcasted_iota(jnp.int32, (channels, channels), 0)
    col_index = lax.broadcasted_iota(jnp.int32, (channels, channels), 1)
    phase = (row_index * col_index % channels).astype(jnp.float32) * (2.0 * math.pi / channels)
    factor = 1.0 / math.sqrt(channels)
    cosine = (jnp.cos(phase) * factor).astype(jnp.bfloat16)
    sine = (jnp.sin(phase) * factor).astype(jnp.bfloat16)
    upper = jnp.concatenate([cosine, -sine], axis=1)
    lower = jnp.concatenate([sine, cosine], axis=1)
    return jnp.concatenate([upper, lower], axis=0)

def reference(voltages, taps):
    volts = voltages.astype(jnp.float32).reshape(2, INPUTS, SPECTRA, C).transpose(2, 1, 0, 3)
    coeffs = taps.astype(jnp.float32) / 1024.0
    padded = jnp.pad(volts, ((TAPS - 1, 0), (0, 0), (0, 0), (0, 0)))
    filtered = jnp.zeros((SPECTRA, INPUTS, 2, C), jnp.float32)
    for tap in range(TAPS):
        filtered = filtered + coeffs[tap][None, None, None, :] * padded[tap:tap + SPECTRA]
    weighted = lax.optimization_barrier(filtered.astype(jnp.bfloat16)).astype(jnp.float32)
    table = dft_table(C).astype(jnp.float32)
    spectra = jnp.dot(weighted.reshape(SPECTRA * INPUTS, 2 * C), table, precision=lax.Precision.HIGHEST, preferred_element_type=jnp.float32)
    spectra = lax.optimization_barrier(spectra.astype(jnp.bfloat16)).astype(jnp.float32)
    group = C // N_FREQ
    blocks = spectra.reshape(SPECTRA, INPUTS, 2, N_FREQ, group).transpose(3, 0, 1, 2, 4)
    factor = 1.0 / math.sqrt(SPECTRA)

    def correlate(tile):
        rotated = jnp.stack([-tile[:, :, 1], tile[:, :, 0]], axis=2)
        partner = jnp.stack([tile, rotated], axis=2)
        return jnp.einsum('sirc,sjorc->ocij', tile, partner, precision=lax.Precision.HIGHEST) * factor
    result = lax.map(correlate, blocks)
    return result.transpose(1, 0, 2, 3, 4).reshape(2, C, INPUTS, INPUTS)
```

```python
import functools
import math

import jax
import jax.numpy as jnp
import numpy as np
from jax import lax
from jax.experimental import pallas as pl
from jax.experimental.pallas import tpu as pltpu
from jax.sharding import PartitionSpec as P

LATE_CHUNKS = 2
EARLY_CHUNKS = 4
MIB = 1 << 20


def swapped(value, axis, distance):
    pairs = [(i, i ^ distance) for i in range(lax.axis_size(axis))]
    return lax.ppermute(value, axis, pairs)


def from_behind(value, axis):
    pairs = [(i, i + 1) for i in range(lax.axis_size(axis) - 1)]
    return lax.ppermute(value, axis, pairs)


def dft_rows(channels, groups, chunks):
    n = np.arange(channels, dtype=np.int64)
    phase = ((n[:, None] * n[None, :]) % channels).astype(np.float32)
    phase = phase * np.float32(2.0 * math.pi / channels)
    factor = np.float32(1.0 / math.sqrt(channels))
    cosine = np.cos(phase.astype(np.float64)).astype(np.float32) * factor
    sine = np.sin(phase.astype(np.float64)).astype(np.float32) * factor
    real = np.concatenate([cosine, sine], axis=1)
    imag = np.concatenate([-sine, cosine], axis=1)
    rows = np.stack([real, imag]).astype(jnp.bfloat16)
    size = channels // groups // chunks
    rows = rows.reshape(2, groups, chunks, size, 2 * channels).transpose(2, 1, 0, 3, 4)
    return [rows[c].reshape(groups * 2 * size, 2 * channels) for c in range(chunks)]


def weigh(taps_ref, *refs):
    *parts, out_ref = refs
    channels = taps_ref.shape[1]
    frames = []
    for ref in parts:
        for f in range(ref.shape[2] // channels):
            frames.append((ref, f * channels))
    ntaps = taps_ref.shape[0]
    count = out_ref.shape[0]
    frames = frames[len(frames) - (count + ntaps - 1):]
    coeffs = taps_ref[...].astype(jnp.float32) * (1.0 / 1024.0)
    for part in range(2):
        held = [ref[part, :, at:at + channels].astype(jnp.float32) for ref, at in frames]
        for s in range(count):
            total = coeffs[0:1] * held[s]
            for t in range(1, ntaps):
                total = total + coeffs[t:t + 1] * held[s + t]
            out_ref[s, :, part * channels:(part + 1) * channels] = total.astype(jnp.bfloat16)


def weighted_spectra(taps, sources, count):
    channels = taps.shape[1]
    inputs = sources[0][0].shape[1]
    step = min(16, inputs)
    specs = [pl.BlockSpec(taps.shape, lambda i: (0, 0))]
    for array, at, width in sources:
        specs.append(pl.BlockSpec((2, step, width), lambda i, at=at: (0, i, at)))
    moved = sum(2 * inputs * w * a.dtype.itemsize for a, _, w in sources)
    return pl.pallas_call(
        weigh,
        out_shape=jax.ShapeDtypeStruct((count, inputs, 2 * channels), jnp.bfloat16),
        grid=(inputs // step,),
        in_specs=specs,
        out_specs=pl.BlockSpec((count, step, 2 * channels), lambda i: (0, i, 0)),
        cost_estimate=pl.CostEstimate(
            flops=count * inputs * channels * 16, bytes_accessed=moved + count * inputs * channels * 4, transcendentals=0
        ),
        compiler_params=pltpu.CompilerParams(vmem_limit_bytes=40 * MIB),
    )(taps, *[a for a, _, _ in sources])


def transform(weighted_ref, table_ref, out_ref, turned_ref):
    count, inputs, depth = weighted_ref.shape
    groups, pairs = out_ref.shape[0], out_ref.shape[1]
    size = 2 * pairs
    weighted = weighted_ref[...].reshape(count * inputs, depth)
    result = lax.dot_general(
        table_ref[...], weighted, (((1,), (1,)), ((), ())), preferred_element_type=jnp.float32
    )
    for g in range(groups):
        for part in range(2):
            base = (g * 2 + part) * size
            for s in range(count):
                turned_ref[g, :, part * count + s, :] = result[base:base + size, s * inputs:(s + 1) * inputs]
    out_ref[...] = turned_ref[...].reshape(groups, pairs, 4 * count, inputs).astype(jnp.bfloat16)


def spectra_of(weighted, table, groups):
    count, inputs, depth = weighted.shape
    size = table.shape[0] // groups // 2
    together = max(1, min(groups, 256 // (2 * size)))
    rows = together * 2 * size
    return pl.pallas_call(
        transform,
        out_shape=jax.ShapeDtypeStruct((groups, size // 2, 4 * count, inputs), jnp.bfloat16),
        grid=(groups // together,),
        in_specs=[
            pl.BlockSpec(weighted.shape, lambda g: (0, 0, 0)),
            pl.BlockSpec((rows, depth), lambda g: (g, 0)),
        ],
        out_specs=pl.BlockSpec((together, size // 2, 4 * count, inputs), lambda g: (g, 0, 0, 0)),
        scratch_shapes=[pltpu.VMEM((together, size, 2 * count, inputs), jnp.float32)],
        cost_estimate=pl.CostEstimate(
            flops=2 * table.shape[0] * depth * count * inputs, bytes_accessed=table.size * 2 + weighted.size * 4, transcendentals=0
        ),
        compiler_params=pltpu.CompilerParams(vmem_limit_bytes=40 * MIB),
    )(weighted, table)


def correlate(factor, blocks, me_ref, *refs):
    late, early = refs[:blocks], refs[blocks:2 * blocks]
    out_ref = refs[-1]
    groups, pairs, rows, inputs = late[0].shape
    half = rows // 2
    offsets = [
        pl.multiple_of(jnp.bitwise_xor(me_ref[0], q) * inputs, inputs) for q in range(blocks)
    ]
    sign = jnp.where(
        lax.broadcasted_iota(jnp.int32, (2 * groups, half, inputs), 1) < half // 2, factor, -factor
    ).astype(jnp.float32)

    def pair(p, carry):
        loaded = []
        for q in range(blocks):
            a = late[q][:, p].astype(jnp.float32).reshape(groups, 2, half, inputs)
            b = early[q][:, p].astype(jnp.float32).reshape(groups, 2, half, inputs)
            loaded.append((a, b))
        for h in range(2):
            whole = [jnp.concatenate([a[:, h], b[:, h]], axis=0) for a, b in loaded]
            flat = [w.reshape(2 * groups * half, inputs).astype(jnp.bfloat16) for w in whole]
            rotated = (pltpu.roll(whole[0], half // 2, axis=1) * sign).reshape(2 * groups * half, inputs)
            scaled = (whole[0] * factor).reshape(2 * groups * half, inputs)
            left = jnp.concatenate([scaled, rotated], axis=1).astype(jnp.bfloat16)
            for q in range(blocks):
                product = lax.dot_general(
                    left, flat[q], (((0,), (0,)), ((), ())), preferred_element_type=jnp.float32
                )
                out_ref[0, 2 * p + h, :, pl.ds(offsets[q], inputs)] = product[:inputs]
                out_ref[1, 2 * p + h, :, pl.ds(offsets[q], inputs)] = product[inputs:]
        return carry

    lax.fori_loop(0, pairs, pair, 0)


def correlated(me, late, early, at, late_at, total, factor, visible):
    blocks = len(late)
    groups, pairs, rows, inputs = early[0].shape
    step = min(4, pairs)
    size = 2 * step
    specs = [pl.BlockSpec((groups, step, rows, inputs), lambda i, m: (0, late_at // step + i, 0, 0))] * blocks
    specs += [pl.BlockSpec((groups, step, rows, inputs), lambda i, m: (0, i, 0, 0))] * blocks
    operands = [me, *late, *early]
    aliases = {}
    if visible is not None:
        aliases = {len(operands): 0}
        operands.append(visible)
        specs.append(pl.BlockSpec(memory_space=pl.ANY))
    wide = inputs * blocks
    depth = 2 * groups * rows // 2
    return pl.pallas_call(
        functools.partial(correlate, factor, blocks),
        out_shape=jax.ShapeDtypeStruct((2, total, inputs, wide), jnp.float32),
        grid_spec=pltpu.PrefetchScalarGridSpec(
            num_scalar_prefetch=1,
            grid=(pairs // step,),
            in_specs=specs,
            out_specs=pl.BlockSpec((2, size, inputs, wide), lambda i, m: (0, at // step + i, 0, 0)),
        ),
        input_output_aliases=aliases,
        cost_estimate=pl.CostEstimate(
            flops=2 * 2 * pairs * 2 * inputs * wide * depth, bytes_accessed=2 * pairs * 2 * inputs * wide * 4, transcendentals=0
        ),
        compiler_params=pltpu.CompilerParams(vmem_limit_bytes=48 * MIB),
    )(*operands)


def local(tables, voltages, taps):
    ntaps, channels = taps.shape
    inputs = voltages.shape[1]
    frames = voltages.shape[2] // channels
    groups = lax.axis_size("freq")
    blocks = lax.axis_size("blk")
    group = channels // groups
    early_tables, late_tables = tables
    half = frames // 2
    factor = 1.0 / math.sqrt(frames * groups)
    me = lax.axis_index("blk").astype(jnp.int32).reshape(1)

    tail = voltages[:, :, (frames - ntaps + 1) * channels:].astype(jnp.bfloat16)
    behind = from_behind(tail, "freq")
    late_weighted = weighted_spectra(taps, [(voltages, 0, frames * channels)], half)
    early_weighted = None

    late_sent = [spectra_of(late_weighted, late_tables[0], groups)]
    nlate, nearly = len(late_tables), len(early_tables)
    count = nlate + nearly
    turned = [None] * count
    visible = None
    sent = list(late_sent)
    for step in range(count + 3):
        made = {}
        if step < count:
            made["turn"] = lax.all_to_all(sent[step], "freq", split_axis=0, concat_axis=0, tiled=True)
        if 0 <= step - 1 < count:
            made["far"] = swapped(turned[step - 1][0], "blk", 2)
        if 0 <= step - 2 < count:
            held = turned[step - 2]
            made["near"] = (swapped(held[0], "blk", 1), swapped(held[2], "blk", 1))
        if step + 1 < nlate:
            made["next"] = spectra_of(late_weighted, late_tables[step + 1], groups)
        elif step + 1 < count:
            if early_weighted is None:
                early_weighted = weighted_spectra(
                    taps, [(behind, 0, (ntaps - 1) * channels), (voltages, 0, half * channels)], half
                )
            made["next"] = spectra_of(early_weighted, early_tables[step + 1 - nlate], groups)
        e = step - 3 - nlate
        if e >= 0:
            per = nearly // nlate
            a, b = turned[e // per], turned[nlate + e]
            size = group // nearly // 2
            visible = correlated(
                me, [a[q] for q in range(blocks)], [b[q] for q in range(blocks)],
                e * size, (e % per) * size, group, factor, visible,
            )
            if e + 1 == nearly:
                break
            made["visible"] = visible
        made, turned = lax.optimization_barrier((made, turned))
        visible = made.get("visible", visible)
        if "turn" in made:
            turned[step] = {0: made["turn"]}
        if "far" in made:
            turned[step - 1] = {**turned[step - 1], 2: made["far"]}
        if "near" in made:
            turned[step - 2] = {**turned[step - 2], 1: made["near"][0], 3: made["near"][1]}
        if "next" in made:
            sent.append(made["next"])
    return visible


def solution(mesh):
    groups = mesh.shape["freq"]

    def run(voltages, taps):
        channels = taps.shape[1]
        tables = (
            dft_rows(channels, groups, EARLY_CHUNKS),
            dft_rows(channels, groups, LATE_CHUNKS),
        )
        return jax.shard_map(
            functools.partial(local, tables),
            mesh=mesh,
            in_specs=(P(None, "blk", "freq"), P()),
            out_specs=P(None, "freq", "blk", None),
            check_vma=False,
        )(voltages, taps)

    return run
```

```python
import functools
import math

import jax
import jax.numpy as jnp
import numpy as np
from jax import lax
from jax.experimental import pallas as pl
from jax.experimental.pallas import tpu as pltpu
from jax.sharding import PartitionSpec as P

EARLY = (7, 5, 4)
MIB = 1 << 20
VMEM = 60 * MIB
RATED = 10**11


def swapped(value, axis, distance):
    pairs = [(i, i ^ distance) for i in range(lax.axis_size(axis))]
    return lax.ppermute(value, axis, pairs)


def handed(value, even=True):
    groups, blocks = lax.axis_size("freq"), lax.axis_size("blk")
    pairs = []
    for f in range(groups):
        for k in range(blocks):
            if k % 2 == 1:
                pairs.append((f * blocks + k, (f - 1) % groups * blocks + k))
            elif even and f + 1 < groups:
                pairs.append((f * blocks + k, (f + 1) * blocks + k))
    return lax.ppermute(value, ("freq", "blk"), pairs)


def reached(f, groups, shift, other):
    return (f // 2 + shift) % (groups // 2) * 2 + (f % 2 + other) % 2


def shifted(value, shift, other):
    groups = lax.axis_size("freq")
    pairs = [(f, reached(f, groups, shift, other)) for f in range(groups)]
    return lax.ppermute(value, "freq", pairs)


def cuts(pairs, shares):
    unit = pairs // 16
    ends = [0]
    for share in shares:
        ends.append(ends[-1] + share * unit)
    return ends


def dft_rows(channels, groups, parts):
    n = np.arange(channels, dtype=np.int64)
    phase = ((n[:, None] * n[None, :]) % channels).astype(np.float32)
    phase = phase * np.float32(2.0 * math.pi / channels)
    factor = np.float32(1.0 / math.sqrt(channels))
    cosine = np.cos(phase.astype(np.float64)).astype(np.float32) * factor
    sine = np.sin(phase.astype(np.float64)).astype(np.float32) * factor
    real = np.concatenate([cosine, sine], axis=1)
    imag = np.concatenate([-sine, cosine], axis=1)
    rows = np.stack([real, imag]).astype(jnp.bfloat16)
    rows = rows.reshape(2, groups, channels // groups, 2 * channels).transpose(1, 0, 2, 3)
    return [rows[:, :, 2 * a:2 * b].reshape(groups, -1, 2 * channels) for a, b in parts]


def weigh_frames(taps_ref, frames, out_ref):
    ntaps, channels = taps_ref.shape
    coeffs = taps_ref[...].astype(jnp.float32) * (1.0 / 1024.0)
    for part in range(2):
        held = [frame(part).astype(jnp.float32) for frame in frames]
        for s in range(out_ref.shape[0]):
            total = coeffs[0:1] * held[s]
            for t in range(1, ntaps):
                total = total + coeffs[t:t + 1] * held[s + t]
            out_ref[s, :, part * channels:(part + 1) * channels] = total.astype(jnp.bfloat16)


def frames_of(refs, first, last, channels):
    return [lambda part, f=f: refs[part][0, :, f * channels:(f + 1) * channels] for f in range(first, last)]


def weigh_late(taps_ref, real_ref, imag_ref, out_ref):
    ntaps, channels = taps_ref.shape
    frames = real_ref.shape[2] // channels
    first = frames - out_ref.shape[0] - ntaps + 1
    weigh_frames(taps_ref, frames_of((real_ref, imag_ref), first, frames, channels), out_ref)


def weigh_early(where_ref, taps_ref, real_ref, imag_ref, *refs):
    ntaps, channels = taps_ref.shape
    volts = (real_ref, imag_ref)
    frames = real_ref.shape[2] // channels
    passed, more, out_ref = refs[:2], refs[2:4], refs[4]
    count = out_ref.shape[0]

    @pl.when(where_ref[0] == 0)
    def _():
        before = frames_of(passed, 0, ntaps - 1, channels)
        weigh_frames(taps_ref, before + frames_of(volts, 0, count, channels), out_ref)

    @pl.when(where_ref[0] != 0)
    def _():
        keep = where_ref[1]
        before = [
            lambda part, frame=frame: frame(part) * keep
            for frame in frames_of(volts, frames - ntaps + 1, frames, channels)
        ]
        after = frames_of(passed, 0, ntaps - 1, channels) + frames_of(more, 0, count - ntaps + 1, channels)
        weigh_frames(taps_ref, before + after, out_ref)


def weighted_spectra(taps, voltages, count, where=None, passed=()):
    channels = taps.shape[1]
    _, inputs, samples = voltages.shape
    step = min(64, inputs)
    operands = [taps]
    specs = [pl.BlockSpec(taps.shape, lambda i, *_: (0, 0))]
    for array in (voltages, *passed):
        for part in range(2):
            operands.append(array)
            specs.append(pl.BlockSpec((1, step, array.shape[2]), lambda i, *_, part=part: (part, i, 0)))
    if passed:
        operands = [where, *operands]
    return pl.pallas_call(
        weigh_early if passed else weigh_late,
        out_shape=jax.ShapeDtypeStruct((count, inputs, 2 * channels), jnp.bfloat16),
        grid_spec=pltpu.PrefetchScalarGridSpec(
            num_scalar_prefetch=1 if passed else 0,
            grid=(inputs // step,),
            in_specs=specs,
            out_specs=pl.BlockSpec((count, step, 2 * channels), lambda i, *_: (0, i, 0)),
        ),
        cost_estimate=pl.CostEstimate(
            flops=count * inputs * channels * 16, bytes_accessed=2 * inputs * samples * 4, transcendentals=0
        ),
        compiler_params=pltpu.CompilerParams(vmem_limit_bytes=VMEM),
    )(*operands)


def transform(weighted_ref, table_ref, turned_ref):
    count, inputs, depth = weighted_ref.shape
    groups, rows, _ = table_ref.shape
    size = rows // 2
    weighted = weighted_ref[...].reshape(count * inputs, depth)
    result = lax.dot_general(
        table_ref[...].reshape(groups * rows, depth), weighted, (((1,), (1,)), ((), ())),
        preferred_element_type=jnp.float32,
    )
    for g in range(groups):
        for part in range(2):
            base = g * rows + part * size
            for s in range(count):
                turned_ref[g, :, part * count + s, :] = result[base:base + size, s * inputs:(s + 1) * inputs]


def transform_to(ends, me_ref, weighted_ref, table_ref, *refs):
    *out_refs, turned_ref = refs
    transform(weighted_ref, table_ref, turned_ref)
    low = me_ref[0] % 2
    chunks = len(ends) - 1
    for i in range(len(out_refs) // (2 * chunks)):
        @pl.when(pl.program_id(0) == i)
        def _(i=i):
            for other in range(2):
                source_ref = turned_ref.at[jnp.bitwise_xor(low, other)]
                for c in range(chunks):
                    out_ref = out_refs[(2 * i + other) * chunks + c]
                    value = source_ref[2 * ends[c]:2 * ends[c + 1]]
                    out_ref[...] = value.reshape(out_ref.shape).astype(jnp.bfloat16)


def spectra_to(me, weighted, table, ends):
    count, inputs, depth = weighted.shape
    groups, rows, _ = table.shape
    chunks = len(ends) - 1
    sizes = [b - a for a, b in zip(ends[:-1], ends[1:])]
    shapes = [(size, 4 * count, inputs) for size in sizes] * groups
    made = pl.pallas_call(
        functools.partial(transform_to, ends),
        out_shape=[jax.ShapeDtypeStruct(shape, jnp.bfloat16) for shape in shapes],
        grid_spec=pltpu.PrefetchScalarGridSpec(
            num_scalar_prefetch=1,
            grid=(groups // 2,),
            in_specs=[
                pl.BlockSpec(weighted.shape, lambda i, m: (0, 0, 0)),
                pl.BlockSpec((2, rows, depth), lambda i, m: ((m[0] // 2 + i) % (groups // 2), 0, 0)),
            ],
            out_specs=[pl.BlockSpec(shape, lambda i, m: (0, 0, 0)) for shape in shapes],
            scratch_shapes=[pltpu.VMEM((2, rows // 2, 2 * count, inputs), jnp.float32)],
        ),
        cost_estimate=pl.CostEstimate(
            flops=2 * groups * rows * depth * count * inputs,
            bytes_accessed=groups * rows * depth * 2 + weighted.size * 4,
            transcendentals=0,
        ),
        compiler_params=pltpu.CompilerParams(vmem_limit_bytes=VMEM),
    )(me, weighted, table)
    return [[made[g * chunks + c] for g in range(groups)] for c in range(chunks)]


def transform_by(ends, weighted_ref, table_ref, *refs):
    *out_refs, turned_ref = refs
    transform(weighted_ref, table_ref, turned_ref)
    for c, out_ref in enumerate(out_refs):
        value = turned_ref[:, 2 * ends[c]:2 * ends[c + 1]]
        out_ref[...] = value.reshape(out_ref.shape).astype(jnp.bfloat16)


def spectra_by(weighted, table, ends):
    count, inputs, depth = weighted.shape
    groups, rows, _ = table.shape
    sizes = [b - a for a, b in zip(ends[:-1], ends[1:])]
    some = 4 if rows < 128 * 4 // 3 else 2
    return pl.pallas_call(
        functools.partial(transform_by, ends),
        out_shape=[jax.ShapeDtypeStruct((groups, size, 4 * count, inputs), jnp.bfloat16) for size in sizes],
        grid=(groups // some,),
        in_specs=[
            pl.BlockSpec(weighted.shape, lambda i: (0, 0, 0)),
            pl.BlockSpec((some, rows, depth), lambda i: (i, 0, 0)),
        ],
        out_specs=[pl.BlockSpec((some, size, 4 * count, inputs), lambda i: (i, 0, 0, 0)) for size in sizes],
        scratch_shapes=[pltpu.VMEM((some, rows // 2, 2 * count, inputs), jnp.float32)],
        cost_estimate=pl.CostEstimate(
            flops=2 * groups * rows * depth * count * inputs,
            bytes_accessed=groups * rows * depth * 2 + weighted.size * 4,
            transcendentals=0,
        ),
        compiler_params=pltpu.CompilerParams(vmem_limit_bytes=VMEM),
    )(weighted, table)


def tick(token, *values):
    def body(token_ref, *refs):
        refs[-1][...] = token_ref[...]

    return pl.pallas_call(
        body,
        out_shape=jax.ShapeDtypeStruct(token.shape, token.dtype),
        in_specs=[pl.BlockSpec(token.shape, lambda: (0, 0))] + [pl.BlockSpec(memory_space=pl.ANY)] * len(values),
        out_specs=pl.BlockSpec(token.shape, lambda: (0, 0)),
        cost_estimate=pl.CostEstimate(flops=RATED, bytes_accessed=0, transcendentals=0),
        compiler_params=pltpu.CompilerParams(vmem_limit_bytes=VMEM),
    )(token, *values)


def correlate(factor, distances, nlate, me_ref, order_ref, *refs):
    blocks = len(distances) + 1
    late = [refs[q * nlate:(q + 1) * nlate] for q in range(blocks)]
    early = refs[blocks * nlate:blocks * (nlate + 1)]
    out_ref = refs[-1]
    groups, pairs, rows, inputs = early[0].shape
    half = rows // 2
    width = out_ref.shape[3] // inputs
    at = [jnp.bitwise_xor(me_ref[0], q) for q in distances]
    offsets = [pl.multiple_of(a % width * inputs, inputs) for a in at]
    odd = [a % 2 for a in (me_ref[0], *at)]
    depth = 2 * groups * rows
    sign = jnp.where(
        lax.broadcasted_iota(jnp.int32, (4 * groups, half, inputs), 1) < half // 2, factor, -factor
    ).astype(jnp.float32)
    of_first = lax.broadcasted_iota(jnp.int32, (inputs, depth), 1) % rows < half
    keep = [jnp.where(of_first, 1.0, 0.0).astype(jnp.bfloat16), jnp.where(of_first, 0.0, 1.0).astype(jnp.bfloat16)]

    def pair(p):
        loaded = []
        for q in range(blocks):
            if q and distances[q - 1] == 0:
                loaded.append(loaded[0])
                continue
            tiles = [ref[j, p] for ref in late[q] for j in range(ref.shape[0])]
            tiles += [early[q][order_ref[odd[q], j], p] for j in range(groups)]
            loaded.append(jnp.concatenate(tiles, axis=0))
        own = loaded[0].astype(jnp.float32)
        turned = pltpu.roll(own.reshape(4 * groups, half, inputs), half // 2, axis=1) * sign
        straight = (own * factor).astype(jnp.bfloat16).T
        turned = turned.reshape(depth, inputs).astype(jnp.bfloat16).T
        left = jnp.concatenate([side * mask for mask in keep for side in (straight, turned)], axis=0)
        product = jnp.dot(left, jnp.concatenate(loaded[1:], axis=1), preferred_element_type=jnp.float32)
        for q in range(blocks - 1):
            columns = pl.ds(offsets[q], inputs)
            for h in range(2):
                for part in range(2):
                    at_row = (2 * h + part) * inputs
                    out_ref[part, 2 * p + h, :, columns] = product[at_row:at_row + inputs, q * inputs:(q + 1) * inputs]

    for p in range(pairs):
        pair(p)


def correlated(me, order, held, distances, at, shape, factor, visible, token=None):
    *late, early = held
    groups, pairs, rows, inputs = early[0].shape
    step = math.gcd(4, math.gcd(pairs, at))
    wide = inputs * len(distances)
    operands, specs = [me, order], []
    for q in (0, *distances):
        for array in late:
            operands.append(array[q])
            specs.append(pl.BlockSpec((array[q].shape[0], step, rows, inputs), lambda i, *_: (0, at // step + i, 0, 0)))
    for q in (0, *distances):
        operands.append(early[q])
        specs.append(pl.BlockSpec((groups, step, rows, inputs), lambda i, *_: (0, i, 0, 0)))
    aliases = {}
    if visible is not None:
        aliases = {len(operands): 0}
        operands.append(visible)
        specs.append(pl.BlockSpec(memory_space=pl.ANY))
    if token is not None:
        operands.append(token)
        specs.append(pl.BlockSpec(memory_space=pl.ANY))
    whole = shape[3] == wide
    high = distances[0] // len(distances)
    depth = groups * rows
    return pl.pallas_call(
        functools.partial(correlate, factor, distances, len(late)),
        out_shape=jax.ShapeDtypeStruct(shape, jnp.float32),
        grid_spec=pltpu.PrefetchScalarGridSpec(
            num_scalar_prefetch=2,
            grid=(pairs // step,),
            in_specs=specs,
            out_specs=pl.BlockSpec(
                (2, 2 * step, inputs, wide),
                lambda i, m, _: (0, at // step + i, 0, 0 if whole else jnp.bitwise_xor(m[0] // len(distances), high)),
            ),
        ),
        input_output_aliases=aliases,
        cost_estimate=pl.CostEstimate(
            flops=2 * 2 * pairs * 2 * inputs * wide * depth, bytes_accessed=2 * pairs * 2 * inputs * wide * 4, transcendentals=0
        ),
        compiler_params=pltpu.CompilerParams(vmem_limit_bytes=VMEM),
    )(*operands)


def local(tables, voltages, taps):
    ntaps, channels = taps.shape
    inputs = voltages.shape[1]
    frames = voltages.shape[2] // channels
    groups = lax.axis_size("freq")
    blocks = lax.axis_size("blk")
    group = channels // groups
    ends = cuts(group // 2, EARLY)
    half = frames // 2
    factor = 1.0 / math.sqrt(frames * groups)
    freq = lax.axis_index("freq").astype(jnp.int32)
    blk = lax.axis_index("blk").astype(jnp.int32)
    odd = blk % 2
    me = freq.reshape(1)
    high = groups // 2
    shape = (2, group, inputs, inputs * blocks)
    both = lax.optimization_barrier
    table, first_table, other_table = tables

    begin = jnp.where(odd == 0, frames - ntaps + 1, 0) * channels
    given = lax.dynamic_slice_in_dim(voltages, begin, (ntaps - 1) * channels, 2).astype(jnp.bfloat16)
    more = voltages[:, :, (ntaps - 1) * channels:half * channels].astype(jnp.bfloat16)
    where = jnp.stack([odd, (freq < groups - 1).astype(jnp.int32)])

    passed = [handed(given), handed(more, even=False)]
    (made,) = spectra_to(me, weighted_spectra(taps, voltages, half), table, (0, group // 2))
    near = [made[0]] + [shifted(made[2 * s], s, 0) for s in range(1, high)]
    near, passed, made = both((near, passed, made))

    held = [{0: jnp.stack(near)}]
    far = [shifted(made[2 * s + 1], s, 1) for s in range(high)]
    held[0][2] = swapped(held[0][0], "blk", 2)
    early_weighted = weighted_spectra(taps, voltages, half, where, passed)
    early = spectra_by(early_weighted, first_table, ends[:2])
    held.append({0: jnp.stack(far)})
    held, early, early_weighted = both((held, early, early_weighted))

    index = jnp.arange(groups, dtype=jnp.int32)
    order = jnp.stack([index, (index - 1) % groups])

    nearly = len(ends) - 1
    visible = None
    token = jnp.zeros((8, 128), jnp.float32)
    for step in range(nearly + 2):
        new = {}
        if step < nearly:
            new[step + 2, 0] = lax.all_to_all(early[step], "freq", split_axis=0, concat_axis=0, tiled=True)
        if step <= nearly:
            new[step + 1, 2] = swapped(held[step + 1][0], "blk", 2)
            new[step + 1, 1] = swapped(held[step + 1][0], "blk", 1)
        if step == 0:
            new[0, 1] = swapped(held[0][0], "blk", 1)
            early = early + spectra_by(early_weighted, other_table, [end - ends[1] for end in ends[1:]])
        new[step, 3] = swapped(held[step][2], "blk", 1)
        if step >= 2:
            parts = [held[0], held[1], {**held[step], 3: new[step, 3]}]
            visible = correlated(blk.reshape(1), order, parts, (0, 1, 2, 3), ends[step - 2], shape, factor, visible, token)
        if step < nearly:
            token = tick(token, new[step + 1, 2], *([] if visible is None else [visible]))
        if step == nearly + 1:
            break
        new, held, early, visible, token = both((new, held, early, visible, token))
        held.append({})
        for (c, q), value in new.items():
            held[c][q] = value
    return visible


def solution(mesh):
    groups = mesh.shape["freq"]

    def run(voltages, taps):
        channels = taps.shape[1]
        ends = cuts(channels // groups // 2, EARLY)
        tables = dft_rows(channels, groups, ((0, ends[-1]), (0, ends[1]), (ends[1], ends[-1])))
        return jax.shard_map(
            functools.partial(local, tables),
            mesh=mesh,
            in_specs=(P(None, "blk", "freq"), P()),
            out_specs=P(None, "freq", "blk", None),
            check_vma=False,
        )(voltages, taps)

    return run
```

```python
import functools
import math

import jax
import jax.numpy as jnp
import numpy as np
from jax import lax
from jax.experimental import pallas as pl
from jax.experimental.pallas import tpu as pltpu
from jax.sharding import PartitionSpec as P

EARLY = (6, 5, 5)
MIB = 1 << 20
VMEM = 60 * MIB
RATED = 10**11


def swapped(value, axis, distance):
    pairs = [(i, i ^ distance) for i in range(lax.axis_size(axis))]
    return lax.ppermute(value, axis, pairs)


def handed(value):
    groups, blocks = lax.axis_size("freq"), lax.axis_size("blk")
    pairs = []
    for f in range(groups):
        for k in range(blocks):
            if k % 2 == 1:
                pairs.append((f * blocks + k, (f - 1) % groups * blocks + k))
            elif f + 1 < groups:
                pairs.append((f * blocks + k, (f + 1) * blocks + k))
    return lax.ppermute(value, ("freq", "blk"), pairs)


def reached(f, groups, shift, other):
    return (f // 2 + shift) % (groups // 2) * 2 + (f % 2 + other) % 2


def shifted(value, shift, other):
    groups = lax.axis_size("freq")
    pairs = [(f, reached(f, groups, shift, other)) for f in range(groups)]
    return lax.ppermute(value, "freq", pairs)


def cuts(pairs, shares):
    unit = pairs // 16
    ends = [0]
    for share in shares:
        ends.append(ends[-1] + share * unit)
    return ends


def dft_rows(channels, groups, parts):
    n = np.arange(channels, dtype=np.int64)
    phase = ((n[:, None] * n[None, :]) % channels).astype(np.float32)
    phase = phase * np.float32(2.0 * math.pi / channels)
    factor = np.float32(1.0 / math.sqrt(channels))
    cosine = np.cos(phase.astype(np.float64)).astype(np.float32) * factor
    sine = np.sin(phase.astype(np.float64)).astype(np.float32) * factor
    rows = np.stack([cosine, sine]).astype(jnp.bfloat16)
    rows = rows.reshape(2, groups, channels // groups, channels).transpose(1, 0, 2, 3)
    return [rows[:, :, 2 * a:2 * b].reshape(groups, -1, channels) for a, b in parts]


def weigh_frames(taps_ref, windows, out_ref):
    ntaps, channels = taps_ref.shape
    coeffs = taps_ref[...].astype(jnp.float32) * (1.0 / 1024.0)
    for part in range(2):
        held = {}
        for s, window in enumerate(windows):
            for frame in window:
                if frame not in held:
                    held[frame] = frame(part).astype(jnp.float32)
            total = coeffs[0:1] * held[window[0]]
            for t in range(1, ntaps):
                total = total + coeffs[t:t + 1] * held[window[t]]
            out_ref[s, :, part * channels:(part + 1) * channels] = total.astype(jnp.bfloat16)


def frames_of(refs, first, last, channels):
    return [lambda part, f=f: refs[part][0, :, f * channels:(f + 1) * channels] for f in range(first, last)]


def windows_of(frames, ntaps):
    return [frames[s:s + ntaps] for s in range(len(frames) - ntaps + 1)]


def weigh_late(taps_ref, real_ref, imag_ref, out_ref):
    ntaps, channels = taps_ref.shape
    frames = real_ref.shape[2] // channels
    used = frames_of((real_ref, imag_ref), frames - out_ref.shape[0] - ntaps + 1, frames, channels)
    weigh_frames(taps_ref, windows_of(used, ntaps), out_ref)


def weigh_early(where_ref, taps_ref, real_ref, imag_ref, passed_real_ref, passed_imag_ref, out_ref):
    ntaps, channels = taps_ref.shape
    frames = real_ref.shape[2] // channels
    passed = frames_of((passed_real_ref, passed_imag_ref), 0, ntaps - 1, channels)
    own = frames_of((real_ref, imag_ref), 0, frames, channels)
    count = out_ref.shape[0]

    @pl.when(where_ref[0] == 0)
    def _():
        weigh_frames(taps_ref, windows_of(passed + own[:count], ntaps), out_ref)

    @pl.when(where_ref[0] != 0)
    def _():
        keep = where_ref[1]
        before = [lambda part, frame=frame: frame(part) * keep for frame in own[frames - ntaps + 1:]]
        weigh_frames(taps_ref, windows_of(before + passed, ntaps) + windows_of(own[:count], ntaps), out_ref)


def weighted_spectra(taps, voltages, count, where=None, passed=None):
    channels = taps.shape[1]
    _, inputs, samples = voltages.shape
    step = min(64, inputs)
    operands = [taps]
    specs = [pl.BlockSpec(taps.shape, lambda i, *_: (0, 0))]
    for array in (voltages,) if passed is None else (voltages, passed):
        for part in range(2):
            operands.append(array)
            specs.append(pl.BlockSpec((1, step, array.shape[2]), lambda i, *_, part=part: (part, i, 0)))
    if passed is not None:
        operands = [where, *operands]
    return pl.pallas_call(
        weigh_late if passed is None else weigh_early,
        out_shape=jax.ShapeDtypeStruct((count, inputs, 2 * channels), jnp.bfloat16),
        grid_spec=pltpu.PrefetchScalarGridSpec(
            num_scalar_prefetch=0 if passed is None else 1,
            grid=(inputs // step,),
            in_specs=specs,
            out_specs=pl.BlockSpec((count, step, 2 * channels), lambda i, *_: (0, i, 0)),
        ),
        cost_estimate=pl.CostEstimate(
            flops=count * inputs * channels * 16, bytes_accessed=2 * inputs * samples * 4, transcendentals=0
        ),
        compiler_params=pltpu.CompilerParams(vmem_limit_bytes=VMEM),
    )(*operands)


def transform(weighted_ref, table_ref, turned_ref):
    count, inputs, _ = weighted_ref.shape
    groups, rows, depth = table_ref.shape
    size = rows // 2
    table = table_ref[...].reshape(groups * rows, depth)
    real, imag = [
        lax.dot_general(
            table, weighted_ref[:, :, part * depth:(part + 1) * depth].reshape(count * inputs, depth),
            (((1,), (1,)), ((), ())), preferred_element_type=jnp.float32,
        )
        for part in range(2)
    ]
    for g in range(groups):
        cosine, sine = slice(g * rows, g * rows + size), slice(g * rows + size, (g + 1) * rows)
        for s in range(count):
            of = slice(s * inputs, (s + 1) * inputs)
            turned_ref[g, :, s, :] = real[cosine, of] + imag[sine, of]
            turned_ref[g, :, count + s, :] = imag[cosine, of] - real[sine, of]


def transform_to(me_ref, weighted_ref, table_ref, *refs):
    *out_refs, turned_ref = refs
    transform(weighted_ref, table_ref, turned_ref)
    for i, out_ref in enumerate(out_refs):
        @pl.when(pl.program_id(0) == i)
        def _(out_ref=out_ref):
            out_ref[...] = turned_ref[...].reshape(out_ref.shape).astype(jnp.bfloat16)


def spectra_to(me, weighted, table, other):
    count, inputs, _ = weighted.shape
    groups, rows, depth = table.shape
    shifts = groups // 2
    shape = (rows // 4, 4 * count, inputs)
    return pl.pallas_call(
        transform_to,
        out_shape=[jax.ShapeDtypeStruct(shape, jnp.bfloat16)] * shifts,
        grid_spec=pltpu.PrefetchScalarGridSpec(
            num_scalar_prefetch=1,
            grid=(shifts,),
            in_specs=[
                pl.BlockSpec(weighted.shape, lambda i, m: (0, 0, 0)),
                pl.BlockSpec((1, rows, depth), lambda i, m: (reached(m[0], groups, i, other), 0, 0)),
            ],
            out_specs=[pl.BlockSpec(shape, lambda i, m: (0, 0, 0))] * shifts,
            scratch_shapes=[pltpu.VMEM((1, rows // 2, 2 * count, inputs), jnp.float32)],
        ),
        cost_estimate=pl.CostEstimate(
            flops=2 * groups * rows * depth * count * inputs,
            bytes_accessed=groups * rows * depth + weighted.size * 3,
            transcendentals=0,
        ),
        compiler_params=pltpu.CompilerParams(vmem_limit_bytes=VMEM),
    )(me, weighted, table)


def transform_by(ends, weighted_ref, table_ref, *refs):
    *out_refs, turned_ref = refs
    transform(weighted_ref, table_ref, turned_ref)
    for c, out_ref in enumerate(out_refs):
        value = turned_ref[:, 2 * ends[c]:2 * ends[c + 1]]
        out_ref[...] = value.reshape(out_ref.shape).astype(jnp.bfloat16)


def spectra_by(weighted, table, ends):
    count, inputs, _ = weighted.shape
    groups, rows, depth = table.shape
    sizes = [b - a for a, b in zip(ends[:-1], ends[1:])]
    some = 4 if rows < 128 * 4 // 3 else 2
    return pl.pallas_call(
        functools.partial(transform_by, ends),
        out_shape=[jax.ShapeDtypeStruct((groups, size, 4 * count, inputs), jnp.bfloat16) for size in sizes],
        grid=(groups // some,),
        in_specs=[
            pl.BlockSpec(weighted.shape, lambda i: (0, 0, 0)),
            pl.BlockSpec((some, rows, depth), lambda i: (i, 0, 0)),
        ],
        out_specs=[pl.BlockSpec((some, size, 4 * count, inputs), lambda i: (i, 0, 0, 0)) for size in sizes],
        scratch_shapes=[pltpu.VMEM((some, rows // 2, 2 * count, inputs), jnp.float32)],
        cost_estimate=pl.CostEstimate(
            flops=4 * groups * rows * depth * count * inputs,
            bytes_accessed=groups * rows * depth * 2 + weighted.size * 4,
            transcendentals=0,
        ),
        compiler_params=pltpu.CompilerParams(vmem_limit_bytes=VMEM),
    )(weighted, table)


def tick(token, *values):
    def body(token_ref, *refs):
        refs[-1][...] = token_ref[...]

    return pl.pallas_call(
        body,
        out_shape=jax.ShapeDtypeStruct(token.shape, token.dtype),
        in_specs=[pl.BlockSpec(token.shape, lambda: (0, 0))] + [pl.BlockSpec(memory_space=pl.ANY)] * len(values),
        out_specs=pl.BlockSpec(token.shape, lambda: (0, 0)),
        cost_estimate=pl.CostEstimate(flops=RATED, bytes_accessed=0, transcendentals=0),
        compiler_params=pltpu.CompilerParams(vmem_limit_bytes=VMEM),
    )(token, *values)


def correlate(factor, distances, nlate, ntaps, me_ref, *refs):
    blocks = len(distances)
    late = [refs[q * nlate:(q + 1) * nlate] for q in range(blocks)]
    early = refs[blocks * nlate:blocks * (nlate + 1)]
    out_ref = refs[-1]
    groups, pairs, rows, inputs = early[0].shape
    half = rows // 2
    depth = 2 * groups * rows
    sign = jnp.where(
        lax.broadcasted_iota(jnp.int32, (4 * groups, half, inputs), 1) < half // 2, factor, -factor
    ).astype(jnp.float32)
    of_first = lax.broadcasted_iota(jnp.int32, (inputs, depth), 1) % rows < half
    keep = [jnp.where(of_first, 1.0, 0.0).astype(jnp.bfloat16), jnp.where(of_first, 0.0, 1.0).astype(jnp.bfloat16)]

    ahead = lax.broadcasted_iota(jnp.int32, (rows, inputs), 0) % (half // 2) < ntaps - 1
    ahead, level = [jnp.where(ahead, a, 1.0 - a).astype(jnp.bfloat16) for a in (1.0, 0.0)]

    def pair(p, mine):
        loaded = []
        for q in range(blocks):
            tiles = [ref[j, p] for ref in late[q] for j in range(ref.shape[0])]
            for j in range(groups):
                if (mine ^ distances[q]) % 2 == 0:
                    tiles.append(early[q][j, p])
                else:
                    tiles.append(early[q][(j - 1) % groups, p] * ahead + early[q][j, p] * level)
            loaded.append(jnp.concatenate(tiles, axis=0))
        own = loaded[0].astype(jnp.float32)
        turned = pltpu.roll(own.reshape(4 * groups, half, inputs), half // 2, axis=1) * sign
        straight = (own * factor).astype(jnp.bfloat16).T
        turned = turned.reshape(depth, inputs).astype(jnp.bfloat16).T
        left = jnp.concatenate([side * mask for mask in keep for side in (straight, turned)], axis=0)
        product = jnp.dot(left, jnp.concatenate(loaded, axis=1), preferred_element_type=jnp.float32)
        for q in range(blocks):
            first = (mine ^ distances[q]) * inputs
            for h in range(2):
                for part in range(2):
                    block = product[(2 * h + part) * inputs:(2 * h + part + 1) * inputs, q * inputs:(q + 1) * inputs]
                    out_ref[part, 2 * p + h, :, first:first + inputs] = block

    for mine in range(blocks):
        @pl.when(me_ref[0] == mine)
        def _(mine=mine):
            for p in range(pairs):
                pair(p, mine)


def correlated(me, held, distances, at, shape, factor, ntaps, visible, token=None):
    *late, early = held
    groups, pairs, rows, inputs = early[0].shape
    step = math.gcd(4, math.gcd(pairs, at))
    wide = inputs * len(distances)
    operands, specs = [me], []
    for q in distances:
        for array in late:
            operands.append(array[q])
            specs.append(pl.BlockSpec((array[q].shape[0], step, rows, inputs), lambda i, *_: (0, at // step + i, 0, 0)))
    for q in distances:
        operands.append(early[q])
        specs.append(pl.BlockSpec((groups, step, rows, inputs), lambda i, *_: (0, i, 0, 0)))
    aliases = {}
    if visible is not None:
        aliases = {len(operands): 0}
        operands.append(visible)
        specs.append(pl.BlockSpec(memory_space=pl.ANY))
    if token is not None:
        operands.append(token)
        specs.append(pl.BlockSpec(memory_space=pl.ANY))
    depth = groups * rows
    return pl.pallas_call(
        functools.partial(correlate, factor, distances, len(late), ntaps),
        out_shape=jax.ShapeDtypeStruct(shape, jnp.float32),
        grid_spec=pltpu.PrefetchScalarGridSpec(
            num_scalar_prefetch=1,
            grid=(pairs // step,),
            in_specs=specs,
            out_specs=pl.BlockSpec(
                (2, 2 * step, inputs, wide), lambda i, *_: (0, at // step + i, 0, 0)
            ),
        ),
        input_output_aliases=aliases,
        cost_estimate=pl.CostEstimate(
            flops=2 * 2 * pairs * 2 * inputs * wide * depth, bytes_accessed=2 * pairs * 2 * inputs * wide * 4, transcendentals=0
        ),
        compiler_params=pltpu.CompilerParams(vmem_limit_bytes=VMEM),
    )(*operands)


def local(tables, voltages, taps):
    ntaps, channels = taps.shape
    inputs = voltages.shape[1]
    frames = voltages.shape[2] // channels
    groups = lax.axis_size("freq")
    blocks = lax.axis_size("blk")
    group = channels // groups
    ends = cuts(group // 2, EARLY)
    half = frames // 2
    factor = 1.0 / math.sqrt(frames * groups)
    freq = lax.axis_index("freq").astype(jnp.int32)
    blk = lax.axis_index("blk").astype(jnp.int32)
    odd = blk % 2
    me = freq.reshape(1)
    high = groups // 2
    shape = (2, group, inputs, inputs * blocks)
    both = lax.optimization_barrier
    table, first_table, other_table = tables

    begin = jnp.where(odd == 0, frames - ntaps + 1, 0) * channels
    given = lax.dynamic_slice_in_dim(voltages, begin, (ntaps - 1) * channels, 2).astype(jnp.bfloat16)
    where = jnp.stack([odd, (freq < groups - 1).astype(jnp.int32)])

    passed = handed(given)
    weighted = weighted_spectra(taps, voltages, half)
    made = spectra_to(me, weighted, table, 0)
    near = [made[0]] + [shifted(made[shift], shift, 0) for shift in range(1, high)]
    made = spectra_to(me, weighted, table, 1)
    near, passed, made = both((near, passed, made))

    held = [{0: jnp.stack(near)}]
    far = [shifted(made[shift], shift, 1) for shift in range(high)]
    held[0][2] = swapped(held[0][0], "blk", 2)
    early_weighted = weighted_spectra(taps, voltages, half, where, passed)
    early = spectra_by(early_weighted, first_table, ends[:2])
    held.append({0: jnp.stack(far)})
    held, early, early_weighted = both((held, early, early_weighted))

    nearly = len(ends) - 1
    visible = None
    token = jnp.zeros((8, 128), jnp.float32)
    for step in range(nearly + 2):
        new = {}
        if step < nearly:
            new[step + 2, 0] = lax.all_to_all(early[step], "freq", split_axis=0, concat_axis=0, tiled=True)
        if step <= nearly:
            new[step + 1, 2] = swapped(held[step + 1][0], "blk", 2)
            new[step + 1, 1] = swapped(held[step + 1][0], "blk", 1)
        if step == 0:
            new[0, 1] = swapped(held[0][0], "blk", 1)
            early = early + spectra_by(early_weighted, other_table, [end - ends[1] for end in ends[1:]])
        new[step, 3] = swapped(held[step][2], "blk", 1)
        if step >= 2:
            parts = [held[0], held[1], {**held[step], 3: new[step, 3]}]
            visible = correlated(blk.reshape(1), parts, (0, 1, 2, 3), ends[step - 2], shape, factor, ntaps, visible, token)
        if step < nearly:
            token = tick(token, new[step + 1, 2], *([] if visible is None else [visible]))
        if step == nearly + 1:
            break
        new, held, early, visible, token = both((new, held, early, visible, token))
        held.append({})
        for (c, q), value in new.items():
            held[c][q] = value
    return visible


def solution(mesh):
    groups = mesh.shape["freq"]

    def run(voltages, taps):
        channels = taps.shape[1]
        ends = cuts(channels // groups // 2, EARLY)
        tables = dft_rows(channels, groups, ((0, ends[-1]), (0, ends[1]), (ends[1], ends[-1])))
        return jax.shard_map(
            functools.partial(local, tables),
            mesh=mesh,
            in_specs=(P(None, "blk", "freq"), P()),
            out_specs=P(None, "freq", "blk", None),
            check_vma=False,
        )(voltages, taps)

    return run
```

```python
import functools
import math

import jax
import jax.numpy as jnp
import numpy as np
from jax import lax
from jax.experimental import pallas as pl
from jax.experimental.pallas import tpu as pltpu
from jax.sharding import PartitionSpec as P

EARLY = (7, 5, 4)
MIB = 1 << 20
VMEM = 60 * MIB
RATED = 10**11


def swapped(value, axis, distance):
    pairs = [(i, i ^ distance) for i in range(lax.axis_size(axis))]
    return lax.ppermute(value, axis, pairs)


def handed(value):
    groups, blocks = lax.axis_size("freq"), lax.axis_size("blk")
    pairs = []
    for f in range(groups):
        for k in range(blocks):
            if k % 2 == 1:
                pairs.append((f * blocks + k, (f - 1) % groups * blocks + k))
            elif f + 1 < groups:
                pairs.append((f * blocks + k, (f + 1) * blocks + k))
    return lax.ppermute(value, ("freq", "blk"), pairs)


def reached(f, groups, shift, other):
    return (f // 2 + shift) % (groups // 2) * 2 + (f % 2 + other) % 2


def shifted(value, shift, other):
    groups = lax.axis_size("freq")
    pairs = [(f, reached(f, groups, shift, other)) for f in range(groups)]
    return lax.ppermute(value, "freq", pairs)


def cuts(pairs, shares):
    unit = pairs // 16
    ends = [0]
    for share in shares:
        ends.append(ends[-1] + share * unit)
    return ends


def dft_rows(channels, groups, parts):
    n = np.arange(channels, dtype=np.int64)
    phase = ((n[:, None] * n[None, :]) % channels).astype(np.float32)
    phase = phase * np.float32(2.0 * math.pi / channels)
    factor = np.float32(1.0 / math.sqrt(channels))
    cosine = np.cos(phase.astype(np.float64)).astype(np.float32) * factor
    sine = np.sin(phase.astype(np.float64)).astype(np.float32) * factor
    rows = np.stack([cosine, sine]).astype(jnp.bfloat16)
    rows = rows.reshape(2, groups, channels // groups, channels).transpose(1, 0, 2, 3)
    return [rows[:, :, 2 * a:2 * b].reshape(groups, -1, channels) for a, b in parts]


def weigh_frames(taps_ref, windows, out_ref):
    ntaps, channels = taps_ref.shape
    coeffs = taps_ref[...].astype(jnp.float32) * (1.0 / 1024.0)
    for part in range(2):
        held = {}
        for s, window in enumerate(windows):
            for frame in window:
                if frame not in held:
                    held[frame] = frame(part).astype(jnp.float32)
            total = coeffs[0:1] * held[window[0]]
            for t in range(1, ntaps):
                total = total + coeffs[t:t + 1] * held[window[t]]
            out_ref[s, :, part * channels:(part + 1) * channels] = total.astype(jnp.bfloat16)


def frames_of(refs, first, last, channels):
    return [lambda part, f=f: refs[part][0, :, f * channels:(f + 1) * channels] for f in range(first, last)]


def windows_of(frames, ntaps):
    return [frames[s:s + ntaps] for s in range(len(frames) - ntaps + 1)]


def weigh_late(taps_ref, real_ref, imag_ref, out_ref):
    ntaps, channels = taps_ref.shape
    frames = real_ref.shape[2] // channels
    used = frames_of((real_ref, imag_ref), frames - out_ref.shape[0] - ntaps + 1, frames, channels)
    weigh_frames(taps_ref, windows_of(used, ntaps), out_ref)


def weigh_early(where_ref, taps_ref, real_ref, imag_ref, passed_real_ref, passed_imag_ref, out_ref):
    ntaps, channels = taps_ref.shape
    frames = real_ref.shape[2] // channels
    passed = frames_of((passed_real_ref, passed_imag_ref), 0, ntaps - 1, channels)
    own = frames_of((real_ref, imag_ref), 0, frames, channels)
    count = out_ref.shape[0]

    @pl.when(where_ref[0] == 0)
    def _():
        weigh_frames(taps_ref, windows_of(passed + own[:count], ntaps), out_ref)

    @pl.when(where_ref[0] != 0)
    def _():
        keep = where_ref[1]
        before = [lambda part, frame=frame: frame(part) * keep for frame in own[frames - ntaps + 1:]]
        weigh_frames(taps_ref, windows_of(before + passed, ntaps) + windows_of(own[:count], ntaps), out_ref)


def weighted_spectra(taps, voltages, count, where=None, passed=None):
    channels = taps.shape[1]
    _, inputs, samples = voltages.shape
    step = min(64, inputs)
    operands = [taps]
    specs = [pl.BlockSpec(taps.shape, lambda i, *_: (0, 0))]
    for array in (voltages,) if passed is None else (voltages, passed):
        for part in range(2):
            operands.append(array)
            specs.append(pl.BlockSpec((1, step, array.shape[2]), lambda i, *_, part=part: (part, i, 0)))
    if passed is not None:
        operands = [where, *operands]
    return pl.pallas_call(
        weigh_late if passed is None else weigh_early,
        out_shape=jax.ShapeDtypeStruct((count, inputs, 2 * channels), jnp.bfloat16),
        grid_spec=pltpu.PrefetchScalarGridSpec(
            num_scalar_prefetch=0 if passed is None else 1,
            grid=(inputs // step,),
            in_specs=specs,
            out_specs=pl.BlockSpec((count, step, 2 * channels), lambda i, *_: (0, i, 0)),
        ),
        cost_estimate=pl.CostEstimate(
            flops=count * inputs * channels * 16, bytes_accessed=2 * inputs * samples * 4, transcendentals=0
        ),
        compiler_params=pltpu.CompilerParams(vmem_limit_bytes=VMEM if passed is None else 32 * MIB),
    )(*operands)


def transform(weighted_ref, table_ref, turned_ref):
    count, inputs, _ = weighted_ref.shape
    groups, rows, depth = table_ref.shape
    size = rows // 2
    table = table_ref[...].reshape(groups * rows, depth)
    real, imag = [
        lax.dot_general(
            table, weighted_ref[:, :, part * depth:(part + 1) * depth].reshape(count * inputs, depth),
            (((1,), (1,)), ((), ())), preferred_element_type=jnp.float32,
        )
        for part in range(2)
    ]
    for g in range(groups):
        cosine, sine = slice(g * rows, g * rows + size), slice(g * rows + size, (g + 1) * rows)
        for s in range(count):
            of = slice(s * inputs, (s + 1) * inputs)
            turned_ref[g, :, s, :] = real[cosine, of] + imag[sine, of]
            turned_ref[g, :, count + s, :] = imag[cosine, of] - real[sine, of]


def transform_to(me_ref, weighted_ref, table_ref, *refs):
    *out_refs, turned_ref = refs
    transform(weighted_ref, table_ref, turned_ref)
    for i, out_ref in enumerate(out_refs):
        @pl.when(pl.program_id(0) == i)
        def _(out_ref=out_ref):
            out_ref[...] = turned_ref[...].reshape(out_ref.shape).astype(jnp.bfloat16)


def spectra_to(me, weighted, table, other):
    count, inputs, _ = weighted.shape
    groups, rows, depth = table.shape
    shifts = groups // 2
    shape = (rows // 4, 4 * count, inputs)
    return pl.pallas_call(
        transform_to,
        out_shape=[jax.ShapeDtypeStruct(shape, jnp.bfloat16)] * shifts,
        grid_spec=pltpu.PrefetchScalarGridSpec(
            num_scalar_prefetch=1,
            grid=(shifts,),
            in_specs=[
                pl.BlockSpec(weighted.shape, lambda i, m: (0, 0, 0)),
                pl.BlockSpec((1, rows, depth), lambda i, m: (reached(m[0], groups, i, other), 0, 0)),
            ],
            out_specs=[pl.BlockSpec(shape, lambda i, m: (0, 0, 0))] * shifts,
            scratch_shapes=[pltpu.VMEM((1, rows // 2, 2 * count, inputs), jnp.float32)],
        ),
        cost_estimate=pl.CostEstimate(
            flops=2 * groups * rows * depth * count * inputs,
            bytes_accessed=groups * rows * depth + weighted.size * 3,
            transcendentals=0,
        ),
        compiler_params=pltpu.CompilerParams(vmem_limit_bytes=VMEM),
    )(me, weighted, table)


def transform_by(ends, weighted_ref, table_ref, *refs):
    *out_refs, turned_ref = refs
    transform(weighted_ref, table_ref, turned_ref)
    for c, out_ref in enumerate(out_refs):
        value = turned_ref[:, 2 * ends[c]:2 * ends[c + 1]]
        out_ref[...] = value.reshape(out_ref.shape).astype(jnp.bfloat16)


def spectra_by(weighted, table, ends):
    count, inputs, _ = weighted.shape
    groups, rows, depth = table.shape
    sizes = [b - a for a, b in zip(ends[:-1], ends[1:])]
    some = 4 if rows < 128 * 4 // 3 else 2
    return pl.pallas_call(
        functools.partial(transform_by, ends),
        out_shape=[jax.ShapeDtypeStruct((groups, size, 4 * count, inputs), jnp.bfloat16) for size in sizes],
        grid=(groups // some,),
        in_specs=[
            pl.BlockSpec(weighted.shape, lambda i: (0, 0, 0)),
            pl.BlockSpec((some, rows, depth), lambda i: (i, 0, 0)),
        ],
        out_specs=[pl.BlockSpec((some, size, 4 * count, inputs), lambda i: (i, 0, 0, 0)) for size in sizes],
        scratch_shapes=[pltpu.VMEM((some, rows // 2, 2 * count, inputs), jnp.float32)],
        cost_estimate=pl.CostEstimate(
            flops=4 * groups * rows * depth * count * inputs,
            bytes_accessed=groups * rows * depth * 2 + weighted.size * 4,
            transcendentals=0,
        ),
        compiler_params=pltpu.CompilerParams(vmem_limit_bytes=32 * MIB),
    )(weighted, table)


def tick(token, *values):
    def body(token_ref, *refs):
        refs[-1][...] = token_ref[...]

    return pl.pallas_call(
        body,
        out_shape=jax.ShapeDtypeStruct(token.shape, token.dtype),
        in_specs=[pl.BlockSpec(token.shape, lambda: (0, 0))] + [pl.BlockSpec(memory_space=pl.ANY)] * len(values),
        out_specs=pl.BlockSpec(token.shape, lambda: (0, 0)),
        cost_estimate=pl.CostEstimate(flops=RATED, bytes_accessed=0, transcendentals=0),
        compiler_params=pltpu.CompilerParams(vmem_limit_bytes=VMEM),
    )(token, *values)


def correlate(factor, distances, nlate, ntaps, me_ref, *refs):
    blocks = len(distances)
    late = [refs[q * nlate:(q + 1) * nlate] for q in range(blocks)]
    early = refs[blocks * nlate:blocks * (nlate + 1)]
    out_ref = refs[-1]
    groups, pairs, rows, inputs = early[0].shape
    half = rows // 2
    depth = 2 * groups * rows
    sign = jnp.where(
        lax.broadcasted_iota(jnp.int32, (4 * groups, half, inputs), 1) < half // 2, factor, -factor
    ).astype(jnp.float32)
    of_first = lax.broadcasted_iota(jnp.int32, (inputs, depth), 1) % rows < half
    keep = [jnp.where(of_first, 1.0, 0.0).astype(jnp.bfloat16), jnp.where(of_first, 0.0, 1.0).astype(jnp.bfloat16)]

    ahead = lax.broadcasted_iota(jnp.int32, (rows, inputs), 0) % (half // 2) < ntaps - 1
    ahead, level = [jnp.where(ahead, a, 1.0 - a).astype(jnp.bfloat16) for a in (1.0, 0.0)]

    def pair(p, mine):
        loaded = []
        for q in range(blocks):
            tiles = [ref[j, p] for ref in late[q] for j in range(ref.shape[0])]
            for j in range(groups):
                if (mine ^ distances[q]) % 2 == 0:
                    tiles.append(early[q][j, p])
                else:
                    tiles.append(early[q][(j - 1) % groups, p] * ahead + early[q][j, p] * level)
            loaded.append(jnp.concatenate(tiles, axis=0))
        own = loaded[0].astype(jnp.float32)
        turned = pltpu.roll(own.reshape(4 * groups, half, inputs), half // 2, axis=1) * sign
        straight = (own * factor).astype(jnp.bfloat16).T
        turned = turned.reshape(depth, inputs).astype(jnp.bfloat16).T
        left = jnp.concatenate([side * mask for mask in keep for side in (straight, turned)], axis=0)
        product = jnp.dot(left, jnp.concatenate(loaded, axis=1), preferred_element_type=jnp.float32)
        for q in range(blocks):
            first = (mine ^ distances[q]) * inputs
            for h in range(2):
                for part in range(2):
                    block = product[(2 * h + part) * inputs:(2 * h + part + 1) * inputs, q * inputs:(q + 1) * inputs]
                    out_ref[part, 2 * p + h, :, first:first + inputs] = block

    for mine in range(blocks):
        @pl.when(me_ref[0] == mine)
        def _(mine=mine):
            for p in range(pairs):
                pair(p, mine)


def correlated(me, held, distances, at, shape, factor, ntaps, visible, token=None):
    *late, early = held
    groups, pairs, rows, inputs = early[0].shape
    step = math.gcd(4, math.gcd(pairs, at))
    wide = inputs * len(distances)
    operands, specs = [me], []
    for q in distances:
        for array in late:
            operands.append(array[q])
            specs.append(pl.BlockSpec((array[q].shape[0], step, rows, inputs), lambda i, *_: (0, at // step + i, 0, 0)))
    for q in distances:
        operands.append(early[q])
        specs.append(pl.BlockSpec((groups, step, rows, inputs), lambda i, *_: (0, i, 0, 0)))
    aliases = {}
    if visible is not None:
        aliases = {len(operands): 0}
        operands.append(visible)
        specs.append(pl.BlockSpec(memory_space=pl.ANY))
    if token is not None:
        operands.append(token)
        specs.append(pl.BlockSpec(memory_space=pl.ANY))
    depth = groups * rows
    return pl.pallas_call(
        functools.partial(correlate, factor, distances, len(late), ntaps),
        out_shape=jax.ShapeDtypeStruct(shape, jnp.float32),
        grid_spec=pltpu.PrefetchScalarGridSpec(
            num_scalar_prefetch=1,
            grid=(pairs // step,),
            in_specs=specs,
            out_specs=pl.BlockSpec(
                (2, 2 * step, inputs, wide), lambda i, *_: (0, at // step + i, 0, 0)
            ),
        ),
        input_output_aliases=aliases,
        cost_estimate=pl.CostEstimate(
            flops=2 * 2 * pairs * 2 * inputs * wide * depth, bytes_accessed=2 * pairs * 2 * inputs * wide * 4, transcendentals=0
        ),
        compiler_params=pltpu.CompilerParams(vmem_limit_bytes=36 * MIB),
    )(*operands)


def local(tables, voltages, taps):
    ntaps, channels = taps.shape
    inputs = voltages.shape[1]
    frames = voltages.shape[2] // channels
    groups = lax.axis_size("freq")
    blocks = lax.axis_size("blk")
    group = channels // groups
    ends = cuts(group // 2, EARLY)
    half = frames // 2
    factor = 1.0 / math.sqrt(frames * groups)
    freq = lax.axis_index("freq").astype(jnp.int32)
    blk = lax.axis_index("blk").astype(jnp.int32)
    odd = blk % 2
    me = freq.reshape(1)
    high = groups // 2
    shape = (2, group, inputs, inputs * blocks)
    both = lax.optimization_barrier
    table, first_table, other_table = tables

    begin = jnp.where(odd == 0, frames - ntaps + 1, 0) * channels
    given = lax.dynamic_slice_in_dim(voltages, begin, (ntaps - 1) * channels, 2).astype(jnp.bfloat16)
    where = jnp.stack([odd, (freq < groups - 1).astype(jnp.int32)])

    passed = handed(given)
    weighted = weighted_spectra(taps, voltages, half)
    made = spectra_to(me, weighted, table, 0)
    near = [made[0]] + [shifted(made[shift], shift, 0) for shift in range(1, high)]
    made = spectra_to(me, weighted, table, 1)
    near, passed, made = both((near, passed, made))

    held = [{0: jnp.stack(near)}]
    far = [shifted(made[shift], shift, 1) for shift in range(high)]
    held[0][2] = swapped(held[0][0], "blk", 2)
    early_weighted = weighted_spectra(taps, voltages, half, where, passed)
    early = spectra_by(early_weighted, first_table, ends[:2])
    held.append({0: jnp.stack(far)})
    held, early, early_weighted = both((held, early, early_weighted))

    nearly = len(ends) - 1
    visible = None
    token = jnp.zeros((8, 128), jnp.float32)
    for step in range(nearly + 2):
        new = {}
        if step < nearly:
            new[step + 2, 0] = lax.all_to_all(early[step], "freq", split_axis=0, concat_axis=0, tiled=True)
        if step <= nearly:
            new[step + 1, 2] = swapped(held[step + 1][0], "blk", 2)
            new[step + 1, 1] = swapped(held[step + 1][0], "blk", 1)
        if step == 0:
            new[0, 1] = swapped(held[0][0], "blk", 1)
            early = early + spectra_by(early_weighted, other_table, [end - ends[1] for end in ends[1:]])
        new[step, 3] = swapped(held[step][2], "blk", 1)
        if step >= 2:
            parts = [held[0], held[1], {**held[step], 3: new[step, 3]}]
            visible = correlated(blk.reshape(1), parts, (0, 1, 2, 3), ends[step - 2], shape, factor, ntaps, visible, token)
        if step < nearly - 1:
            token = tick(token, new[step + 1, 2], *([] if visible is None else [visible]))
        if step == nearly + 1:
            break
        new, held, early, visible, token = both((new, held, early, visible, token))
        held.append({})
        for (c, q), value in new.items():
            held[c][q] = value
    return visible


def solution(mesh):
    groups = mesh.shape["freq"]

    def run(voltages, taps):
        channels = taps.shape[1]
        ends = cuts(channels // groups // 2, EARLY)
        tables = dft_rows(channels, groups, ((0, ends[-1]), (0, ends[1]), (ends[1], ends[-1])))
        return jax.shard_map(
            functools.partial(local, tables),
            mesh=mesh,
            in_specs=(P(None, "blk", "freq"), P()),
            out_specs=P(None, "freq", "blk", None),
            check_vma=False,
        )(voltages, taps)

    return run
```
